32 devices in a mesh: groups: 1, row: 32 (over z, y, x, core), col: 1.
Axes of the slice: x: 2, y: 2, z: 4, core: 2. Of those that a mesh axis runs over, the one named last changes fastest.
Arguments:
- pair: bfloat16 [128, 128, 128], P(('groups', 'row'), 'col'), may hold values from -6 to 6
- token_mask: int32 [128], P('groups'), may hold values 0 or 1
- norm_gain: float32 [128], replicated, may hold values from 0.1 to 1.9
- norm_bias: float32 [128], replicated, may hold values from -3 to 3
- proj_weight: bfloat16 [128, 256], replicated, may hold values from -0.5 to 0.5
- gate_weight: bfloat16 [128, 128], replicated, may hold values from -0.5 to 0.5
- out_gain: float32 [64], replicated, may hold values from 0.1 to 1.9
- out_weight: bfloat16 [64, 128], replicated, may hold values from -0.75 to 0.75
Outputs:
- update: bfloat16 [128, 128, 128], P(('groups', 'row'), 'col')
The draws below stay inside these ranges and needn't reach their ends.
All inputs are finite; a program needn't handle non-finite values.
Results may differ from the reference program's by a relative error of at most 0.0055.
Values may be sent and summed in bfloat16 or wider, within the bound.
No kernel may reach another device: no remote copies, remote signals or barrier semaphores. Data moves between devices by JAX's collectives and lax.ppermute only.
A program may use at most 64 MiB of HBM per device.

```python
import jax
import jax.numpy as jnp
from jax import lax

C = 128
CH = 64
RT = 4
TOKENS = 128
N_ROW = 32


def plant(result, key, smallest, largest):
    index_at = [jax.random.randint(jax.random.fold_in(key, axis), (), 0, length) for axis, length in enumerate(result.shape)]
    longest = result.shape.index(max(result.shape))
    neighbour = index_at[:longest] + [(index_at[longest] + 1) % result.shape[longest]] + index_at[longest + 1:]
    return result.at[tuple(index_at)].set(smallest).at[tuple(neighbour)].set(largest)


def block_levels(rng, shape, split, low, top_value):
    factor_of, own = 1.0, jax.random.fold_in(rng, 6)
    for position, blocks in split:
        draws = jnp.exp(jax.random.uniform(jax.random.fold_in(own, position), (blocks,), jnp.float32, low / len(split), top_value / len(split)))
        factor_of = factor_of * jnp.repeat(draws, shape[position] // blocks).reshape([-1 if axis == position else 1 for axis in range(len(shape))])
    return factor_of


def gaussian(own_key, shape, deviation, reach, shards=(), kind=jnp.bfloat16):
    array = jax.random.normal(own_key, shape, jnp.float32) * deviation
    if len(shards) > 0:
        array = block_levels(own_key, shape, shards, -0.22, 0.18) * array
    return jnp.clip(array, min=-reach, max=reach).astype(kind)


def setup_inputs(seed: int = 0, part: int = 0) -> dict:
    keys = jax.random.split(jax.random.key(seed), 9)
    part_splits = jax.random.split(jax.random.fold_in(keys[8], part), 9)
    return {
        "pair": gaussian(part_splits[0], (TOKENS, TOKENS, C), 1.0, 6.0, ((0, 32),)),
        "token_mask": plant((jax.random.randint(part_splits[1], (TOKENS,), 0, 8) < 7).astype(jnp.int32), jax.random.fold_in(part_splits[1], 1), 0, 1),
        "norm_gain": jnp.clip(1.0 + 0.18 * jax.random.normal(keys[2], (C,), jnp.float32), 0.1, 1.9),
        "norm_bias": gaussian(keys[3], (C,), 0.5, 3.0, (), jnp.float32),
        "proj_weight": gaussian(keys[4], (C, 4 * CH), C ** -0.5, 0.5),
        "gate_weight": gaussian(keys[5], (C, C), C ** -0.5, 0.5),
        "out_gain": jnp.clip(1.0 + 0.18 * jax.random.normal(keys[6], (CH,), jnp.float32), 0.1, 1.9),
        "out_weight": gaussian(keys[7], (CH, C), CH ** -0.5, 0.75),
    }


def layer_norm(values, gain, bias, axis):
    mean = lax.optimization_barrier(jnp.mean(values, axis=axis, keepdims=True))
    spread = lax.optimization_barrier(jnp.mean(jnp.square(values - mean), axis=axis, keepdims=True))
    return (values - mean) * lax.rsqrt(spread + 1e-05) * gain + bias

def reference(pair, token_mask, norm_gain, norm_bias, proj_weight, gate_weight, out_gain, out_weight):
    keep_token = token_mask.astype(jnp.float32)
    blocks = pair.reshape(N_ROW, RT, TOKENS, C)
    keep_blocks = keep_token.reshape(N_ROW, RT)

    def sides(operands):
        block, keep_rows = operands
        normed = layer_norm(block.astype(jnp.float32), norm_gain, norm_bias, -1).astype(jnp.bfloat16)
        proj = jnp.dot(normed.reshape(RT * TOKENS, C), proj_weight, preferred_element_type=jnp.float32)
        proj = proj.reshape(RT, TOKENS, 4 * CH)
        keep = (keep_rows[:, None] * keep_token[None, :])[:, :, None]
        left = (keep * jax.nn.sigmoid(proj[:, :, CH:2 * CH]) * proj[:, :, :CH]).astype(jnp.bfloat16)
        right = (keep * jax.nn.sigmoid(proj[:, :, 3 * CH:]) * proj[:, :, 2 * CH:3 * CH]).astype(jnp.bfloat16)
        return (left, right)
    left, right = lax.map(sides, (blocks, keep_blocks))
    left = left.reshape(TOKENS, TOKENS, CH).transpose(2, 0, 1)
    right = right.reshape(TOKENS, TOKENS, CH).transpose(2, 0, 1)

    def channel(operands):
        left_one, right_one = operands
        return jnp.dot(left_one.astype(jnp.float32), right_one.astype(jnp.float32).T, precision=lax.Precision.HIGHEST)
    tri = lax.map(channel, (left, right))
    tri_blocks = tri.reshape(CH, N_ROW, RT, TOKENS).transpose(1, 0, 2, 3)

    def finish(operands):
        block, tri_block = operands
        normed = layer_norm(block.astype(jnp.float32), norm_gain, norm_bias, -1).astype(jnp.bfloat16)
        flat = normed.reshape(RT * TOKENS, C)
        tri_normed = layer_norm(tri_block, out_gain[:, None, None], 0.0, 0).astype(jnp.bfloat16)
        projected = jnp.dot(tri_normed.reshape(CH, RT * TOKENS).T, out_weight, preferred_element_type=jnp.float32)
        gate = jax.nn.sigmoid(jnp.dot(flat, gate_weight, preferred_element_type=jnp.float32))
        return (gate * projected).astype(jnp.bfloat16).reshape(RT, TOKENS, C)
    update = lax.map(finish, (blocks, tri_blocks))
    return update.reshape(TOKENS, TOKENS, C)
```

```python
import math

import jax
import jax.numpy as jnp
from jax import lax
from jax.sharding import PartitionSpec as P


def layer_norm(values, gain, axis):
    mean = jnp.mean(values, axis=axis, keepdims=True)
    spread = jnp.mean(jnp.square(values - mean), axis=axis, keepdims=True)
    return (values - mean) * lax.rsqrt(spread + 1e-05) * gain


def local(pair, token_mask, norm_gain, norm_bias, proj_weight, gate_weight, out_gain, out_weight):
    tok_rows, tok_cols, channels = pair.shape
    width = out_weight.shape[0]
    devices = lax.axis_size("row")
    owners = math.gcd(devices, width)
    spare = devices // owners
    mine = width // owners
    row = lax.axis_index("row")
    normed = (layer_norm(pair.astype(jnp.float32), norm_gain, -1) + norm_bias).astype(jnp.bfloat16)
    flat = normed.reshape(tok_rows * tok_cols, channels)
    proj = jnp.einsum("pc,cw->wp", flat, proj_weight, preferred_element_type=jnp.float32)
    keep_token = token_mask.astype(jnp.float32)
    keep_rows = lax.dynamic_slice_in_dim(keep_token, row * tok_rows, tok_rows)
    keep_cols = lax.dynamic_slice_in_dim(keep_token, lax.axis_index("col") * tok_cols, tok_cols)
    keep = (keep_rows[:, None] * keep_cols[None, :]).reshape(1, tok_rows * tok_cols)
    left = (keep * jax.nn.sigmoid(proj[width : 2 * width]) * proj[:width]).astype(jnp.bfloat16)
    right = (keep * jax.nn.sigmoid(proj[3 * width :]) * proj[2 * width : 3 * width]).astype(
        jnp.bfloat16
    )
    sides = jnp.stack(
        [
            left.reshape(owners, mine, tok_rows, tok_cols),
            right.reshape(owners, mine, tok_rows, tok_cols),
        ],
        axis=1,
    )
    if spare > 1:
        sides = jnp.repeat(sides, spare, axis=0)
    got = lax.all_to_all(sides, "row", 0, 0)
    gate = jax.nn.sigmoid(jnp.dot(flat, gate_weight, preferred_element_type=jnp.float32))
    got = got.reshape(owners, spare, 2, mine, tok_rows, tok_cols)
    left_all = lax.dynamic_index_in_dim(got[:, :, 0], row % spare, axis=1, keepdims=False)
    left_all = left_all.transpose(1, 0, 2, 3).reshape(mine, owners * tok_rows, tok_cols)
    right_all = got[:, :, 1].transpose(2, 0, 1, 3, 4).reshape(mine, devices * tok_rows, tok_cols)
    tri = jnp.einsum("cik,cjk->cij", left_all, right_all, preferred_element_type=jnp.float32)
    tri = lax.psum_scatter(tri, "col", scatter_dimension=2, tiled=True).astype(jnp.bfloat16)
    back = tri.reshape(mine, owners, tok_rows, tok_cols).transpose(1, 0, 2, 3)
    groups = [[owner * spare + part for owner in range(owners)] for part in range(spare)]
    home = lax.all_to_all(back, "row", 0, 0, axis_index_groups=groups if spare > 1 else None)
    home = home.reshape(width, tok_rows * tok_cols).astype(jnp.float32)
    tri_normed = layer_norm(home, out_gain[:, None], 0).astype(jnp.bfloat16)
    projected = jnp.einsum("cp,cd->pd", tri_normed, out_weight, preferred_element_type=jnp.float32)
    return (gate * projected).astype(jnp.bfloat16).reshape(tok_rows, tok_cols, channels)


def solution(mesh):
    placed = (P(("groups", "row"), "col", None), P("groups"), P(), P(), P(), P(), P(), P())
    return jax.shard_map(
        local,
        mesh=mesh,
        in_specs=placed,
        out_specs=P(("groups", "row"), "col", None),
        check_vma=False,
    )
```

```python
import jax
import jax.numpy as jnp
from jax import lax
from jax.sharding import PartitionSpec as P


def layer_norm(values, gain, axis):
    mean = jnp.mean(values, axis=axis, keepdims=True)
    spread = jnp.mean(jnp.square(values - mean), axis=axis, keepdims=True)
    return (values - mean) * lax.rsqrt(spread + 1e-05) * gain


def local(pair, token_mask, norm_gain, norm_bias, proj_weight, gate_weight, out_gain, out_weight):
    tok_rows, tok_cols, channels = pair.shape
    width = out_weight.shape[0]
    row = lax.axis_index("row")
    normed = (layer_norm(pair.astype(jnp.float32), norm_gain, -1) + norm_bias).astype(jnp.bfloat16)
    flat = normed.reshape(tok_rows * tok_cols, channels)
    keep_token = token_mask.astype(jnp.float32)
    keep_rows = lax.dynamic_slice_in_dim(keep_token, row * tok_rows, tok_rows)
    keep_cols = lax.dynamic_slice_in_dim(keep_token, lax.axis_index("col") * tok_cols, tok_cols)
    keep = (keep_rows[:, None] * keep_cols[None, :]).reshape(1, tok_rows * tok_cols)

    def side(weight):
        proj = jnp.einsum("pc,cw->wp", flat, weight, preferred_element_type=jnp.float32)
        gated = (keep * jax.nn.sigmoid(proj[width:]) * proj[:width]).astype(jnp.bfloat16)
        return gated.reshape(width, tok_rows, tok_cols)

    right = lax.all_gather(side(proj_weight[:, 2 * width :]), "row", axis=0)
    left = side(proj_weight[:, : 2 * width])
    gate = jax.nn.sigmoid(jnp.dot(flat, gate_weight, preferred_element_type=jnp.float32))
    right = right.transpose(1, 0, 2, 3).reshape(width, -1, tok_cols)
    tri = jnp.einsum("cik,cjk->cij", left, right, preferred_element_type=jnp.float32)
    tri = lax.psum_scatter(tri, "col", scatter_dimension=2, tiled=True)
    tri = tri.reshape(width, tok_rows * tok_cols)
    tri_normed = layer_norm(tri, out_gain[:, None], 0).astype(jnp.bfloat16)
    projected = jnp.einsum("cp,cd->pd", tri_normed, out_weight, preferred_element_type=jnp.float32)
    return (gate * projected).astype(jnp.bfloat16).reshape(tok_rows, tok_cols, channels)


def solution(mesh):
    placed = (P(("groups", "row"), "col", None), P("groups"), P(), P(), P(), P(), P(), P())
    return jax.shard_map(
        local,
        mesh=mesh,
        in_specs=placed,
        out_specs=P(("groups", "row"), "col", None),
        check_vma=False,
    )
```

```python
import functools

import jax
import jax.numpy as jnp
from jax import lax
from jax.experimental import pallas as pl
from jax.experimental.pallas import tpu as pltpu
from jax.sharding import PartitionSpec as P

GROUP = 8
LANES = 128
LIMIT = pltpu.CompilerParams(vmem_limit_bytes=8 * 2**20)


def layer_norm(values, gain, axis):
    mean = jnp.mean(values, axis=axis, keepdims=True)
    spread = jnp.mean(jnp.square(values - mean), axis=axis, keepdims=True)
    return (values - mean) * lax.rsqrt(spread + 1e-05) * gain


def contract(one, other, one_axis, other_axis):
    dims = (((one_axis,), (other_axis,)), ((), ()))
    return lax.dot_general(one, other, dims, preferred_element_type=jnp.float32)


class Plan:
    def __init__(self):
        self.devices = lax.axis_size("row")
        chip_bits = self.devices.bit_length() - 2
        self.left_bits = max(0, (chip_bits - 2) // 2)
        self.right_bits = chip_bits - self.left_bits
        left_low = lax.axis_size("col") > 1
        self.left_shift = 0 if left_low else self.right_bits
        self.right_shift = self.left_bits if left_low else 0
        rest = sorted(range(2, 1 << self.right_bits), key=lambda e: (-e.bit_count(), -e))
        self.slots = list(zip(rest[1::2], rest[0::2]))

    def lefts(self):
        return 1 << self.left_bits

    def rights(self):
        return 1 << self.right_bits

    def own(self):
        chip = lax.axis_index("row") // 2
        return chip >> self.left_shift & self.lefts() - 1, chip >> self.right_shift & self.rights() - 1

    def permute(self, value, even, odd):
        pairs = [(one, one ^ (odd if one % 2 else even)) for one in range(self.devices)]
        return lax.ppermute(value, "row", pairs)

    def swap(self, value):
        return self.permute(value, 1, 1)

    def send_left(self, value, d):
        move = d << 1 + self.left_shift
        return self.permute(value, move, move)

    def send_right(self, value, even, odd):
        shift = 1 + self.right_shift
        return self.permute(value, even << shift, odd << shift)


def project_kernel(*refs):
    sources, (normed_ref, left_ref, right_ref) = refs[:5], refs[5:8]
    held, arrived = refs[8:13], refs[13]
    copies = [
        pltpu.make_async_copy(source, to, arrived.at[n])
        for n, (source, to) in enumerate(zip(sources, held))
    ]
    for copy in copies:
        copy.start()
    pair_ref, gain_ref, bias_ref, mask_ref, weight_ref = held
    rows, cols, channels = pair_ref.shape
    width = weight_ref.shape[1] // 4
    total = rows * width
    place = lax.broadcasted_iota(jnp.int32, (total, total), 0)
    source = lax.broadcasted_iota(jnp.int32, (total, total), 1)
    channel = place // rows + GROUP - 1 - 2 * (place // rows % GROUP)
    moves = (source == place % rows * width + channel).astype(jnp.bfloat16)
    for copy in copies[:3]:
        copy.wait()
    pair = pair_ref[...].reshape(rows * cols, channels).astype(jnp.float32)
    normed = (layer_norm(pair, gain_ref[...], -1) + bias_ref[...]).astype(jnp.bfloat16)
    normed_ref[...] = normed
    for copy in copies[3:]:
        copy.wait()
    proj = contract(weight_ref[...], normed, 0, 1)
    keep_token = mask_ref[...].astype(jnp.float32)
    token = lax.broadcasted_iota(jnp.int32, keep_token.shape, 1)
    first_col = pl.multiple_of(lax.axis_index("col") * cols, cols)
    keep_cols = mask_ref[:, pl.ds(first_col, cols)].astype(jnp.float32)
    lefts, rights = [], []
    for r in range(rows):
        at = token == lax.axis_index("row") * rows + r
        keep = keep_cols * jnp.sum(jnp.where(at, keep_token, 0.0), axis=1, keepdims=True)
        part = proj[:, r * cols : (r + 1) * cols]
        lefts.append(keep * jax.nn.sigmoid(part[width : 2 * width]) * part[:width])
        rights.append(keep * jax.nn.sigmoid(part[3 * width :]) * part[2 * width : 3 * width])
    left = [one[c : c + GROUP] for c in range(0, width, GROUP) for one in lefts]
    left_ref[...] = jnp.concatenate(left, axis=0).astype(jnp.bfloat16)
    right = jnp.concatenate(rights, axis=0).astype(jnp.bfloat16)
    right_ref[...] = contract(moves, right, 1, 0).astype(jnp.bfloat16)


def project(pair, token_mask, norm_gain, norm_bias, proj_weight):
    rows, cols, channels = pair.shape
    side = jax.ShapeDtypeStruct((rows * proj_weight.shape[1] // 4, cols), jnp.bfloat16)
    sources = [pair, norm_gain[None], norm_bias[None], token_mask[None], proj_weight]
    return pl.pallas_call(
        project_kernel,
        out_shape=[jax.ShapeDtypeStruct((rows * cols, channels), jnp.bfloat16), side, side],
        in_specs=[pl.BlockSpec(memory_space=pltpu.HBM)] * len(sources),
        scratch_shapes=[pltpu.VMEM(one.shape, one.dtype) for one in sources]
        + [pltpu.SemaphoreType.DMA((len(sources),))],
        compiler_params=LIMIT,
        name="project",
    )(*sources)


def products_kernel(rows, width, slots, lefts, *refs):
    left, (own, near) = refs[:lefts], refs[lefts : lefts + 2]
    fetched = refs[lefts + 2 : lefts + 2 + len(slots)]
    handed = refs[lefts + 2 + len(slots) : lefts + 2 + 2 * len(slots)]
    gain_ref, pieces = refs[lefts + 2 + 2 * len(slots)], refs[lefts + 3 + 2 * len(slots) :]
    part = rows * GROUP
    ahead = LANES // part
    ident = lax.broadcasted_iota(jnp.int32, (width, width), 0) == lax.broadcasted_iota(
        jnp.int32, (width, width), 1
    )
    gain = jnp.sum(jnp.where(ident, gain_ref[...], 0.0), axis=1, keepdims=True)
    slot = lax.broadcasted_iota(jnp.int32, (GROUP, LANES), 1) % part // rows

    def body(core):
        right = {0: (own, core), 1: (near, core)}
        for (even, odd), mine, others in zip(slots, fetched, handed):
            right[even] = (others if core else mine, 0)
            right[odd] = (mine if core else others, 1)
        blocks = range(0, len(right), ahead)
        groups = [[[] for _ in blocks] for _ in left]
        for start in range(0, rows * width, part):
            one = jnp.concatenate([ref[start : start + part] for ref in left], axis=0)
            chosen = []
            for bit in (0, 1):
                for block in blocks:
                    for e in range(ahead):
                        ref, even_at = right[block + (e + 1) % ahead]
                        chosen.append(ref[bit ^ even_at, start : start + part])
            dots = contract(one, jnp.concatenate(chosen, axis=0), 1, 1)
            for q in range(len(left)):
                for n in range(len(blocks)):
                    tile = jnp.zeros((GROUP, LANES), jnp.float32)
                    for r in range(rows):
                        at = (q * rows + r) * GROUP
                        for bit in (0, 1):
                            goal = 2 * r + bit
                            first = (bit * len(blocks) + n) * LANES
                            here = dots[at : at + GROUP, first : first + LANES]
                            moved = pltpu.roll(here, rows * (goal + 1), 1, stride=rows, stride_axis=0)
                            tile = jnp.where(slot == goal, moved, tile)
                    groups[q][n].append(tile)
        for q, piece in enumerate(pieces):
            for n in range(len(blocks)):
                tri = jnp.concatenate(groups[q][n], axis=0)
                piece[:, n * LANES : (n + 1) * LANES] = layer_norm(tri, gain, 0).astype(jnp.bfloat16)

    @pl.when(lax.axis_index("row") % 2 == 0)
    def _():
        body(0)

    @pl.when(lax.axis_index("row") % 2 == 1)
    def _():
        body(1)


def products(plan, left, own, near, fetched, handed, out_gain):
    width = out_gain.shape[0]
    rows = own.shape[1] // width
    piece = jax.ShapeDtypeStruct((width, plan.rights() * 2 * rows * rows), jnp.bfloat16)
    return pl.pallas_call(
        functools.partial(products_kernel, rows, width, plan.slots, len(left)),
        out_shape=[piece] * len(left),
        compiler_params=LIMIT,
        name="products",
    )(*left, own, near, *fetched, *handed, out_gain[None])


def products_any(plan, left, own, near, fetched, handed, out_gain):
    width = out_gain.shape[0]
    cols = own.shape[2]
    rows = own.shape[1] // width
    is_even = lax.axis_index("row") % 2 == 0
    right = {0: jnp.where(is_even, own, own[::-1])}
    if near is not None:
        right[1] = jnp.where(is_even, near, near[::-1])
    for (even, odd), mine, others in zip(plan.slots, fetched, handed):
        right[even] = jnp.where(is_even, mine, others)
        right[odd] = jnp.where(is_even, others, mine)[::-1]
    right = jnp.stack([right[e] for e in range(plan.rights())])
    right = jnp.take(right, jnp.arange(plan.rights()) ^ plan.own()[1], axis=0)
    left = jnp.stack(left).reshape(plan.lefts(), width // GROUP, rows, GROUP, cols)
    left = left.transpose(1, 3, 0, 2, 4).reshape(width, -1, cols)
    right = right.reshape(2 * plan.rights(), width // GROUP, GROUP, rows, cols)[:, :, ::-1]
    right = right.transpose(1, 2, 0, 3, 4).reshape(width, -1, cols)
    tri = jnp.einsum("cik,cjk->cij", left, right, preferred_element_type=jnp.float32)
    tri = lax.psum_scatter(tri, "col", scatter_dimension=2, tiled=True)
    normed = layer_norm(tri, out_gain[:, None, None], 0).astype(jnp.bfloat16)
    normed = normed.reshape(width, plan.lefts(), rows, -1, 2 * rows).transpose(1, 0, 3, 2, 4)
    return [one.reshape(width, -1) for one in normed]


def finish_kernel(plan, rows, ordered, *refs):
    homes = refs[:-4]
    gate_ref, weight_ref, out_ref, placed = refs[-4:]
    step = 2 * rows
    cols = out_ref.shape[0] // rows
    left, right = plan.own()
    right = 0 if ordered else right
    for d, home in enumerate(homes):
        projected = contract(home[...], weight_ref[...], 0, 0)
        for e in range(home.shape[1] // (rows * step)):
            chip = ((left ^ d) << plan.left_shift) + ((right ^ e) << plan.right_shift)
            for r in range(rows):
                at = (e * rows + r) * step
                to = pl.multiple_of(r * cols + chip * step, step)
                placed[pl.ds(to, step), :] = projected[at : at + step]
    out_ref[...] = (gate_ref[...] * placed[...]).astype(jnp.bfloat16)


def finish(plan, homes, gate, out_weight, rows, ordered):
    return pl.pallas_call(
        functools.partial(finish_kernel, plan, rows, ordered),
        out_shape=jax.ShapeDtypeStruct(gate.shape, jnp.bfloat16),
        scratch_shapes=[pltpu.VMEM(gate.shape, jnp.float32)],
        compiler_params=LIMIT,
        name="finish",
    )(*homes, gate, out_weight)


def local(pair, token_mask, norm_gain, norm_bias, proj_weight, gate_weight, out_gain, out_weight):
    rows, cols, channels = pair.shape
    plan = Plan()
    normed, mine, right = project(pair, token_mask, norm_gain, norm_bias, proj_weight)
    other = plan.swap(right)
    left = [mine] + [plan.send_left(mine, d) for d in range(1, plan.lefts())]
    own = jnp.stack([right, other])
    fetched = [plan.send_right(own, even, odd) for even, odd in plan.slots]
    near = plan.send_right(own, 1, 1) if plan.rights() > 1 else None
    handed = [plan.swap(one) for one in fetched]
    gate = jax.nn.sigmoid(jnp.dot(normed, gate_weight, preferred_element_type=jnp.float32))
    part = rows * GROUP
    fits = lax.axis_size("col") == 1 and 2 * rows == GROUP and LANES % part == 0
    fits = fits and plan.rights() % (LANES // part) == 0 and cols % LANES == 0
    compute = products if fits else products_any
    pieces = compute(plan, left, own, near, fetched, handed, out_gain)
    homes = [pieces[0]] + [plan.send_left(pieces[d], d) for d in range(1, plan.lefts())]
    update = finish(plan, homes, gate, out_weight, rows, not fits)
    return update.reshape(rows, cols, channels)


def solution(mesh):
    placed = (P(("groups", "row"), "col", None), P("groups"), P(), P(), P(), P(), P(), P())
    return jax.shard_map(
        local,
        mesh=mesh,
        in_specs=placed,
        out_specs=P(("groups", "row"), "col", None),
        check_vma=False,
    )
```
